32 devices in a mesh: section: 8 (over z, y), expert: 4 (over x, core).
Axes of the slice: x: 2, y: 2, z: 4, core: 2. Of those that a mesh axis runs over, the one named last changes fastest.
Arguments:
- carried: bfloat16 [8, 512, 2048], P('section', 'expert'), may hold values from -6 to 6
- halting: int32 [8, 512], P('section', 'expert'), may hold values from 1 to 2
- section_lap: int32 [8], P('section'), may hold values from 1 to 2
- routing: int32 [8, 512, 8], P('section', 'expert'), may hold values from 0 to 63, all different within a row; in each aligned block of 128 rows (0 to 127, 128 to 255, ..., all dimensions but the last counted through in order) at most 24 rows name the same one
- attention_gain: float32 [8, 2048], P('section'), may hold values from 0.25 to 1.75
- attention_in: bfloat16 [8, 2048, 3, 2048], P('section', None, None, 'expert')
- attention_out: bfloat16 [8, 2048, 2048], P('section', 'expert'), may hold values from -0.125 to 0.125
- expert_gain: float32 [8, 2048], P('section'), may hold values from 0.25 to 1.75
- router: bfloat16 [8, 2048, 64], P('section'), may hold values from -0.125 to 0.125
- expert_in: bfloat16 [8, 64, 2048, 256], P('section', 'expert'), may hold values from -0.125 to 0.125
- expert_out: bfloat16 [8, 64, 256, 2048], P('section', 'expert'), may hold values from -0.375 to 0.375
Outputs:
- stepped: bfloat16 [8, 512, 2048], P('section', 'expert')
The draws below stay inside these ranges and needn't reach their ends.
Inputs may be any that keep to these rules, and one draw needn't show every extreme that they name: `routing`: within each aligned block of 128 consecutive tokens of a section's micro-batch, no expert is named by more than 24 tokens, and the 8 experts of one token differ.
All inputs are finite; a program needn't handle non-finite values.
Results may differ from the reference program's by a relative error of at most 0.013.
The reference program's roundings to bfloat16 on the way count: a program that leaves them out, or rounds other values in their place, can miss the bound.
Values may be sent and summed in bfloat16 or wider, within the bound.
A program may use at most 192 MiB of HBM per device.

```python
import math
import jax
import jax.numpy as jnp
import numpy as np
from jax import lax

D = 2048
HEADS = 16
EXPERTS = 64
EXPERT_HID = 256
TOPK = 8
TOK_DEV = 128
HEAD_SIZE = 128
HEAD_GROUP = 4
SEQ_LEN = 512
CAP = 24
N_SECTION = 8
N_EXPERT = 4


def draw_attention_in(key, part):
    key = jax.random.fold_in(key, 7)
    normal_draw = jax.random.truncated_normal(key, -6.0, 6.0, (N_SECTION, D, 3, D), jnp.float32) * D ** (-0.5)
    factor = jnp.array([1.0, 1.0, 3.0], jnp.float32)
    return (normal_draw * factor[None, None, :, None]).astype(jnp.bfloat16)


def place_ends(entries, stream_key, least, largest):
    index_at = [jax.random.randint(jax.random.fold_in(stream_key, axis), (), 0, length) for axis, length in enumerate(entries.shape)]
    widest = entries.shape.index(max(entries.shape))
    next_to = index_at[:widest] + [(index_at[widest] + 1) % entries.shape[widest]] + index_at[widest + 1:]
    return entries.at[tuple(index_at)].set(least).at[tuple(next_to)].set(largest)


def steps_of(own_key, shape, shards, smallest, high):
    loudness = 1.0
    for dim, blocks in shards:
        heights = jax.random.uniform(jax.random.fold_in(jax.random.fold_in(own_key, 6), dim), (blocks,), jnp.float32, smallest / len(shards), high / len(shards))
        loudness = loudness * jnp.repeat(jnp.exp(heights), shape[dim] // blocks).reshape((-1,) + (1,) * (len(shape) - 1 - dim))
    return loudness


def deal_out(own_key, own, number, rows, amount, top, most, lean):
    order = jax.random.permutation(own_key, amount)
    crowded, ordinary = load_shares(amount, rows * top, most, lean, True), load_shares(amount, rows * top, most, lean, False)
    places = jnp.arange(amount)

    def named(tallies, rotation):
        used = int((tallies > 0).sum())
        fixed = max(1, used // 4)
        passed = fixed + (places - fixed + rotation * (used - fixed)) % max(1, amount - fixed)
        return jnp.zeros((amount,), jnp.int32).at[order[jnp.where(places < fixed, places, passed)]].set(jnp.asarray(tallies, jnp.int32))

    tallies = jnp.where(number % 4 == 0, named(crowded, number // 4), named(ordinary, number - number // 4 - 1))
    mixed = jax.random.permutation(jax.random.fold_in(own, 3), amount)
    giver, taker = mixed[0:amount // 2 * 2:2], mixed[1:amount // 2 * 2:2]
    room = jnp.minimum(tallies[giver] - 1, most - tallies[taker]) // 2
    room = jnp.where((giver == order[0]) | (taker == order[0]) | (tallies[taker] == 0), 0, jnp.maximum(room, 0))
    passed = jax.random.randint(jax.random.fold_in(own, 4), (amount // 2,), 0, 1 << 20) % (room + 1)
    tallies = tallies.at[giver].add(-passed).at[taker].add(passed)
    labels = jnp.searchsorted(jnp.cumsum(tallies), jnp.arange(rows * top), side="right").astype(jnp.int32)
    grid = labels.reshape(top, rows).T
    grid = grid[jax.random.permutation(jax.random.fold_in(own, 1), rows)]
    rotation = jax.random.randint(jax.random.fold_in(own, 2), (rows, 1), 0, top)
    return jnp.take_along_axis(grid, (jnp.arange(top)[None, :] + rotation) % top, axis=1)


def load_shares(number_of, total, most, lean, full):
    portions = [(1 << 20) // math.isqrt(standing ** lean) + 1 for standing in range(1, number_of + 1)]
    largest = most if full else min(most, max(-(-total // number_of), total * portions[0] // sum(portions)))
    least = 1 if total - largest >= number_of - 1 else 0
    counts, spare = [largest] + [least] * (number_of - 1), total - largest - least * (number_of - 1)
    while spare > 0:
        candidates = [i for i in range(1, number_of) if counts[i] < largest] or [i for i in range(1, number_of) if counts[i] < most]
        mass, remaining = sum([portions[i] for i in candidates]), spare
        for i in candidates:
            more = min(most - counts[i], max(1, remaining * portions[i] // mass), spare)
            counts[i] = counts[i] + more
            spare = spare - more
    return np.array(counts)


def gaussian(own_key, dims, scale, most, pieces=(), held_as=jnp.bfloat16):
    values = scale * jax.random.normal(own_key, dims, jnp.float32)
    if pieces:
        values = values * steps_of(own_key, dims, pieces, -0.22, 0.18)
    return jnp.clip(values, -most, most).astype(held_as)


def setup_inputs(seed: int = 0) -> dict:
    splits = jax.random.split(jax.random.key(seed), 12)
    carried = gaussian(splits[0], (N_SECTION, SEQ_LEN, D), 1.0, 6.0, ((0, 8), (1, 4)))
    halting = place_ends(jax.random.randint(splits[1], (N_SECTION, SEQ_LEN), 1, 3), jax.random.fold_in(splits[1], 1), 1, 2).astype(jnp.int32)
    section_lap = place_ends(jax.random.randint(splits[2], (N_SECTION,), 1, 3), jax.random.fold_in(splits[2], 1), 1, 2).astype(jnp.int32)
    routing_keys = jax.random.split(jax.random.fold_in(splits[3], 1), N_SECTION * SEQ_LEN // TOK_DEV)
    routing_turns = jax.random.permutation(jax.random.fold_in(splits[3], 3), N_SECTION * SEQ_LEN // TOK_DEV)
    routing = jax.vmap(lambda own, number: deal_out(jax.random.fold_in(splits[3], 2), own, number, TOK_DEV, EXPERTS, TOPK, CAP, 2))(routing_keys, routing_turns).reshape((N_SECTION, SEQ_LEN, TOPK))
    attention_gain = jnp.clip(1.0 + 0.15 * jax.random.normal(splits[4], (N_SECTION, D), jnp.float32), 0.25, 1.75)
    attention_in = draw_attention_in(jax.random.fold_in(splits[11], 71), 0)
    attention_out = gaussian(splits[6], (N_SECTION, D, D), D ** -0.5, 0.125, ((0, 8), (1, 4)))
    expert_gain = jnp.clip(1.0 + 0.15 * jax.random.normal(splits[7], (N_SECTION, D), jnp.float32), 0.25, 1.75)
    router = gaussian(splits[8], (N_SECTION, D, EXPERTS), D ** -0.5, 0.125, ((0, 8),))
    expert_in = gaussian(splits[9], (N_SECTION, EXPERTS, D, EXPERT_HID), D ** -0.5, 0.125, ((0, 8), (1, 4)))
    expert_out = gaussian(splits[10], (N_SECTION, EXPERTS, EXPERT_HID, D), EXPERT_HID ** -0.5, 0.375, ((0, 8), (1, 4)))
    return dict(carried=carried, halting=halting, section_lap=section_lap, routing=routing, attention_gain=attention_gain, attention_in=attention_in, attention_out=attention_out, expert_gain=expert_gain, router=router, expert_in=expert_in, expert_out=expert_out)


EPSILON = 1e-06

def rms_scale(inputs, gain_row):
    mean_sq = lax.optimization_barrier(jnp.mean(inputs * inputs, axis=-1, keepdims=True))
    return inputs * lax.rsqrt(mean_sq + EPSILON) * gain_row

def head_attention(queries, keys_all, values_all):
    scores = jnp.dot(queries, keys_all.T, preferred_element_type=jnp.float32) * HEAD_SIZE ** (-0.5)
    row_ids = lax.broadcasted_iota(jnp.int32, scores.shape, 0)
    col_ids = lax.broadcasted_iota(jnp.int32, scores.shape, 1)
    scores = jnp.where(col_ids <= row_ids, scores, -jnp.inf)
    row_max = lax.optimization_barrier(jnp.max(scores, axis=-1, keepdims=True))
    weights = jnp.exp(scores - row_max)
    weights = (weights / lax.optimization_barrier(jnp.sum(weights, axis=-1, keepdims=True))).astype(jnp.bfloat16)
    return jnp.dot(weights, values_all, preferred_element_type=jnp.float32).astype(jnp.bfloat16)

def block_positions(routes, active, experts_total):
    expert_ids = jnp.arange(experts_total, dtype=jnp.int32)
    one_hot = (routes[:, :, None] == expert_ids).astype(jnp.int32) * active[:, None, None].astype(jnp.int32)
    flat_hot = one_hot.reshape(-1, experts_total)
    before = jnp.cumsum(flat_hot, axis=0) - flat_hot
    return lax.optimization_barrier(jnp.sum(before * flat_hot, axis=1)).reshape(routes.shape).astype(jnp.int32)

def positions_all(routes, active):
    return block_positions(routes, active, EXPERTS)

def one_expert(operands):
    rows_in, weight_in, weight_out = operands
    hidden = jax.nn.relu(jnp.dot(rows_in, weight_in, preferred_element_type=jnp.float32)).astype(jnp.bfloat16)
    return jnp.dot(hidden, weight_out, preferred_element_type=jnp.float32).astype(jnp.bfloat16)

def section_layer(operands):
    incoming, halt_laps, lap_now, routes, attention_gain, attention_in, attention_out, expert_gain, router, expert_in, expert_out = operands
    residual = incoming.astype(jnp.float32)
    normed = rms_scale(residual, attention_gain).astype(jnp.bfloat16)
    projected = jnp.dot(normed, attention_in.reshape(D, 3 * D), preferred_element_type=jnp.float32).astype(jnp.bfloat16)
    projected = projected.reshape(SEQ_LEN, 3, HEADS, HEAD_SIZE)
    out_groups = attention_out.reshape(HEADS // HEAD_GROUP, HEAD_GROUP * HEAD_SIZE, D)

    def one_group(running, group_index):
        first_head = group_index * HEAD_GROUP
        group_cols = lax.dynamic_slice_in_dim(projected, first_head, HEAD_GROUP, 2)
        head_outs = [head_attention(group_cols[:, 0, member], group_cols[:, 1, member], group_cols[:, 2, member]) for member in range(HEAD_GROUP)]
        joined = jnp.concatenate(head_outs, axis=1)
        group_term = jnp.dot(joined, out_groups[group_index], preferred_element_type=jnp.float32).astype(jnp.bfloat16)
        return (running + group_term.astype(jnp.float32), None)
    attention_sum, _ = lax.scan(one_group, jnp.zeros((SEQ_LEN, D), jnp.float32), jnp.arange(HEADS // HEAD_GROUP).astype(jnp.int32))
    updated = residual + attention_sum
    expert_input = rms_scale(updated, expert_gain).astype(jnp.bfloat16)
    active = halt_laps >= lap_now
    gate_all = jax.nn.sigmoid(jnp.dot(expert_input, router, preferred_element_type=jnp.float32))
    gate_vals = jnp.take_along_axis(gate_all, routes, axis=1)
    block_routes = routes.reshape(N_EXPERT, TOK_DEV, TOPK)
    block_active = active.reshape(N_EXPERT, TOK_DEV)
    slot_pos = jax.vmap(positions_all)(block_routes, block_active)
    block_ids = jnp.arange(N_EXPERT).astype(jnp.int32)[:, None, None]
    slot_index = block_routes * (N_EXPERT * CAP) + block_ids * CAP + slot_pos
    slot_index = jnp.where(block_active[:, :, None], slot_index, EXPERTS * N_EXPERT * CAP).reshape(SEQ_LEN, TOPK)
    slot_index = slot_index.astype(jnp.int32)
    copies = jnp.broadcast_to(expert_input[:, None, :], (SEQ_LEN, TOPK, D)).reshape(-1, D)
    buffer = jnp.zeros((EXPERTS * N_EXPERT * CAP, D), jnp.bfloat16).at[slot_index.reshape(-1)].set(copies, mode='drop')
    produced = lax.map(one_expert, (buffer.reshape(EXPERTS, N_EXPERT * CAP, D), expert_in, expert_out)).reshape(-1, D)
    picked = produced[jnp.where(active[:, None], slot_index, 0)]
    weight = jnp.where(active[:, None], gate_vals, 0.0)
    expert_sum = lax.optimization_barrier(jnp.sum(weight[:, :, None] * picked.astype(jnp.float32), axis=1))
    return jnp.where(active[:, None], updated + expert_sum, residual).astype(jnp.bfloat16)

def reference(carried, halting, section_lap, routing, attention_gain, attention_in, attention_out, expert_gain, router, expert_in, expert_out):
    incoming = jnp.roll(carried, 1, axis=0)
    return lax.map(section_layer, (incoming, halting, section_lap, routing, attention_gain, attention_in, attention_out, expert_gain, router, expert_in, expert_out))
```

```python
import jax
import jax.numpy as jnp
from jax import lax
from jax.sharding import PartitionSpec as P

HEAD_SIZE = 128
CAP = 24


EPSILON = 1e-06


def passed_along(block, axis, distance):
    devices = range(lax.axis_size(axis))
    route = [((i - distance) % len(devices), i) for i in devices]
    return lax.ppermute(block, axis, route)


def rms_scale(inputs, gain_row):
    mean_sq = jnp.mean(inputs * inputs, axis=-1, keepdims=True)
    return inputs * lax.rsqrt(mean_sq + EPSILON) * gain_row


def local(
    carried,
    halting,
    section_lap,
    routing,
    attention_gain,
    attention_in,
    attention_out,
    expert_gain,
    router,
    expert_in,
    expert_out,
):
    incoming = passed_along(carried, "section", 1)[0]
    tok_dev = incoming.shape[0]
    model_width = incoming.shape[1]
    groups = lax.axis_size("expert")
    residual = incoming.astype(jnp.float32)
    normed = rms_scale(residual, attention_gain[0]).astype(jnp.bfloat16)
    weights_in = jnp.transpose(attention_in[0], (1, 0, 2))
    head_cols = weights_in.shape[2]
    heads_here = head_cols // HEAD_SIZE
    gathered = lax.all_gather(normed, "expert", axis=0, tiled=True)
    seq_len = gathered.shape[0]
    queries, keys_all, values_all = (
        jnp.dot(gathered, weights_in[part], preferred_element_type=jnp.float32)
        .astype(jnp.bfloat16)
        .reshape(seq_len, heads_here, HEAD_SIZE)
        for part in range(3)
    )
    row_block = min(512, seq_len)

    def attend_block(block_index):
        first_row = block_index * row_block
        query_rows = lax.dynamic_slice_in_dim(queries, first_row, row_block, 0)
        scores = jnp.einsum(
            "qhc,khc->hqk", query_rows, keys_all, preferred_element_type=jnp.float32
        ) * HEAD_SIZE ** (-0.5)
        row_ids = first_row + lax.broadcasted_iota(jnp.int32, (1, row_block, seq_len), 1)
        col_ids = lax.broadcasted_iota(jnp.int32, (1, row_block, seq_len), 2)
        scores = jnp.where(col_ids <= row_ids, scores, -jnp.inf)
        row_max = jnp.max(scores, axis=-1, keepdims=True)
        weights = jnp.exp(scores - row_max)
        weights = (weights / jnp.sum(weights, axis=-1, keepdims=True)).astype(jnp.bfloat16)
        return jnp.einsum(
            "hqk,khc->qhc", weights, values_all, preferred_element_type=jnp.float32
        ).astype(jnp.bfloat16)

    attended = lax.map(attend_block, jnp.arange(seq_len // row_block, dtype=jnp.int32)).reshape(
        seq_len, head_cols
    )
    out_rows = attention_out[0]
    attention_sum = lax.psum_scatter(
        jnp.dot(attended, out_rows, preferred_element_type=jnp.float32).astype(jnp.bfloat16),
        "expert",
        scatter_dimension=0,
        tiled=True,
    ).astype(jnp.float32)
    updated = residual + attention_sum
    expert_input = rms_scale(updated, expert_gain[0]).astype(jnp.bfloat16)
    active = halting[0] >= section_lap[0]
    experts_total = router.shape[2]
    exp_local = expert_in.shape[1]
    routes = jnp.where(active[:, None], routing[0], experts_total).T
    routes_all = lax.all_gather(routes, "expert", axis=0)
    expert_ids = lax.axis_index("expert") * exp_local + jnp.arange(exp_local, dtype=jnp.int32)
    chosen = jnp.any(routes_all[:, :, None, :] == expert_ids[None, None, :, None], axis=1)
    earlier = jnp.triu(jnp.ones((tok_dev, tok_dev), jnp.bfloat16), 1)
    place = jnp.einsum(
        "bet,tu->beu", chosen.astype(jnp.bfloat16), earlier, preferred_element_type=jnp.float32
    ).astype(jnp.int32)
    slots = jnp.where(chosen, place, CAP)[:, :, None, :] == jnp.arange(CAP)[:, None]
    tokens = lax.all_gather(expert_input, "expert", axis=0)
    columns = lax.dynamic_slice_in_dim(router[0].T, expert_ids[0], exp_local, 0)
    gates = jax.nn.sigmoid(
        jnp.einsum("ed,btd->bet", columns, tokens, preferred_element_type=jnp.float32)
    )
    packed = jnp.einsum(
        "bect,btd->ebcd", slots.astype(jnp.bfloat16), tokens, preferred_element_type=jnp.bfloat16
    ).reshape(exp_local, groups * CAP, model_width)
    hidden = jax.nn.relu(
        jnp.einsum("ecd,edh->ech", packed, expert_in[0], preferred_element_type=jnp.float32)
    ).astype(jnp.bfloat16)
    produced = jnp.einsum(
        "ech,ehd->ecd", hidden, expert_out[0], preferred_element_type=jnp.float32
    ).astype(jnp.bfloat16)
    produced = produced.reshape(exp_local, groups, CAP, model_width)
    weight = jnp.where(slots, gates[:, :, None, :], 0.0)
    coarse = lax.reduce_precision(weight, 8, 7)
    fine = (weight - coarse).astype(jnp.bfloat16)
    partial = sum(
        jnp.einsum("bect,ebcd->btd", part, produced, preferred_element_type=jnp.float32)
        for part in (coarse.astype(jnp.bfloat16), fine)
    )
    expert_sum = lax.psum_scatter(
        partial.astype(jnp.bfloat16).reshape(-1, model_width),
        "expert",
        scatter_dimension=0,
        tiled=True,
    ).astype(jnp.float32)
    stepped = jnp.where(active[:, None], updated + expert_sum, residual).astype(jnp.bfloat16)
    return stepped[None]


def solution(mesh):
    in_specs = (
        P("section", "expert", None),
        P("section", "expert"),
        P("section"),
        P("section", "expert", None),
        P("section", None),
        P("section", None, None, "expert"),
        P("section", "expert", None),
        P("section", None),
        P("section", None, None),
        P("section", "expert", None, None),
        P("section", "expert", None, None),
    )
    out_specs = P("section", "expert", None)
    return jax.shard_map(local, mesh=mesh, in_specs=in_specs, out_specs=out_specs, check_vma=False)
```

```python
import jax
import jax.numpy as jnp
from jax import lax
from jax.experimental import pallas as pl
from jax.experimental.pallas import tpu as pltpu
from jax.sharding import PartitionSpec as P

HEAD_SIZE = 128
CAP = 24


EPSILON = 1e-06


def passed_along(block, axis, distance):
    devices = range(lax.axis_size(axis))
    route = [((i - distance) % len(devices), i) for i in devices]
    return lax.ppermute(block, axis, route)


def rms_scale(inputs, gain_row):
    mean_sq = jnp.mean(inputs * inputs, axis=-1, keepdims=True)
    return inputs * lax.rsqrt(mean_sq + EPSILON) * gain_row


def local_general(
    carried,
    halting,
    section_lap,
    routing,
    attention_gain,
    attention_in,
    attention_out,
    expert_gain,
    router,
    expert_in,
    expert_out,
):
    incoming = passed_along(carried, "section", 1)[0]
    tok_dev = incoming.shape[0]
    model_width = incoming.shape[1]
    groups = lax.axis_size("expert")
    residual = incoming.astype(jnp.float32)
    normed = rms_scale(residual, attention_gain[0]).astype(jnp.bfloat16)
    weights_in = jnp.transpose(attention_in[0], (1, 0, 2))
    head_cols = weights_in.shape[2]
    heads_here = head_cols // HEAD_SIZE
    gathered = lax.all_gather(normed, "expert", axis=0, tiled=True)
    seq_len = gathered.shape[0]
    queries, keys_all, values_all = (
        jnp.dot(gathered, weights_in[part], preferred_element_type=jnp.float32)
        .astype(jnp.bfloat16)
        .reshape(seq_len, heads_here, HEAD_SIZE)
        for part in range(3)
    )
    row_block = min(512, seq_len)

    def attend_block(block_index):
        first_row = block_index * row_block
        query_rows = lax.dynamic_slice_in_dim(queries, first_row, row_block, 0)
        scores = jnp.einsum(
            "qhc,khc->hqk", query_rows, keys_all, preferred_element_type=jnp.float32
        ) * HEAD_SIZE ** (-0.5)
        row_ids = first_row + lax.broadcasted_iota(jnp.int32, (1, row_block, seq_len), 1)
        col_ids = lax.broadcasted_iota(jnp.int32, (1, row_block, seq_len), 2)
        scores = jnp.where(col_ids <= row_ids, scores, -jnp.inf)
        row_max = jnp.max(scores, axis=-1, keepdims=True)
        weights = jnp.exp(scores - row_max)
        weights = (weights / jnp.sum(weights, axis=-1, keepdims=True)).astype(jnp.bfloat16)
        return jnp.einsum(
            "hqk,khc->qhc", weights, values_all, preferred_element_type=jnp.float32
        ).astype(jnp.bfloat16)

    attended = lax.map(attend_block, jnp.arange(seq_len // row_block, dtype=jnp.int32)).reshape(
        seq_len, head_cols
    )
    out_rows = attention_out[0]
    attention_sum = lax.psum_scatter(
        jnp.dot(attended, out_rows, preferred_element_type=jnp.float32).astype(jnp.bfloat16),
        "expert",
        scatter_dimension=0,
        tiled=True,
    ).astype(jnp.float32)
    updated = residual + attention_sum
    expert_input = rms_scale(updated, expert_gain[0]).astype(jnp.bfloat16)
    active = halting[0] >= section_lap[0]
    experts_total = router.shape[2]
    exp_local = expert_in.shape[1]
    routes = jnp.where(active[:, None], routing[0], experts_total).T
    routes_all = lax.all_gather(routes, "expert", axis=0)
    expert_ids = lax.axis_index("expert") * exp_local + jnp.arange(exp_local, dtype=jnp.int32)
    chosen = jnp.any(routes_all[:, :, None, :] == expert_ids[None, None, :, None], axis=1)
    earlier = jnp.triu(jnp.ones((tok_dev, tok_dev), jnp.bfloat16), 1)
    place = jnp.einsum(
        "bet,tu->beu", chosen.astype(jnp.bfloat16), earlier, preferred_element_type=jnp.float32
    ).astype(jnp.int32)
    slots = jnp.where(chosen, place, CAP)[:, :, None, :] == jnp.arange(CAP)[:, None]
    tokens = lax.all_gather(expert_input, "expert", axis=0)
    columns = lax.dynamic_slice_in_dim(router[0].T, expert_ids[0], exp_local, 0)
    gates = jax.nn.sigmoid(
        jnp.einsum("ed,btd->bet", columns, tokens, preferred_element_type=jnp.float32)
    )
    packed = jnp.einsum(
        "bect,btd->ebcd", slots.astype(jnp.bfloat16), tokens, preferred_element_type=jnp.bfloat16
    ).reshape(exp_local, groups * CAP, model_width)
    hidden = jax.nn.relu(
        jnp.einsum("ecd,edh->ech", packed, expert_in[0], preferred_element_type=jnp.float32)
    ).astype(jnp.bfloat16)
    produced = jnp.einsum(
        "ech,ehd->ecd", hidden, expert_out[0], preferred_element_type=jnp.float32
    ).astype(jnp.bfloat16)
    produced = produced.reshape(exp_local, groups, CAP, model_width)
    weight = jnp.where(slots, gates[:, :, None, :], 0.0)
    coarse = lax.reduce_precision(weight, 8, 7)
    fine = (weight - coarse).astype(jnp.bfloat16)
    partial = sum(
        jnp.einsum("bect,ebcd->btd", part, produced, preferred_element_type=jnp.float32)
        for part in (coarse.astype(jnp.bfloat16), fine)
    )
    expert_sum = lax.psum_scatter(
        partial.astype(jnp.bfloat16).reshape(-1, model_width),
        "expert",
        scatter_dimension=0,
        tiled=True,
    ).astype(jnp.float32)
    stepped = jnp.where(active[:, None], updated + expert_sum, residual).astype(jnp.bfloat16)
    return stepped[None]


CHUNKS = 4
SLOT = 32
F32 = jnp.float32
BF16 = jnp.bfloat16


def tick_kernel(
    carried, choice, active, gain_a, gain_e, columns, w_in, w_out, e_in, e_out, out,
    vw_in, vw_out, ve_in, ve_out, packed, incoming, tokens, updated, qkv, heads,
    stage, from_sib, from_cnt, weight, choices,
    load_sem, hop_s, hop_r, gather_s, gather_r, sum_s, sum_r, choice_s, choice_r,
):
    me = lax.axis_index("expert")
    section, sections = lax.axis_index("section"), lax.axis_size("section")
    sib = me + 1 - 2 * lax.rem(me, 2)
    cnt = me + 2 - 4 * (me // 2)
    dia = sib + 2 - 4 * (sib // 2)
    after, ahead = lax.rem(section + 1, sections), lax.rem(section + sections - 1, sections)
    exp_local, width = e_in.shape[0], e_in.shape[1]
    rows = tokens.shape[2]
    block = CHUNKS * rows

    loads = [
        pltpu.make_async_copy(w_in, vw_in, load_sem.at[0]),
        pltpu.make_async_copy(w_out, vw_out, load_sem.at[1]),
        pltpu.make_async_copy(e_in, ve_in, load_sem.at[2]),
        pltpu.make_async_copy(e_out, ve_out, load_sem.at[3]),
    ]
    loads[0].start()
    loads[1].start()

    barrier = pltpu.get_barrier_semaphore()
    for peer in (sib, cnt, dia):
        pl.semaphore_signal(barrier, inc=1, device_id={"expert": peer})
    for peer in (after, ahead):
        pl.semaphore_signal(barrier, inc=1, device_id={"section": peer})
    pl.semaphore_wait(barrier, 5)

    hops = [
        pltpu.make_async_remote_copy(
            src_ref=carried.at[c], dst_ref=incoming.at[c], send_sem=hop_s.at[c],
            recv_sem=hop_r.at[c], device_id={"section": after},
        )
        for c in range(CHUNKS)
    ]
    for hop in hops:
        hop.start()
    shared = []
    for i, peer in enumerate((sib, cnt, dia)):
        shared.append(
            pltpu.make_async_remote_copy(
                src_ref=choice, dst_ref=choices.at[me], send_sem=choice_s.at[i],
                recv_sem=choice_r.at[i], device_id={"expert": peer},
            )
        )
        shared[-1].start()
    choices[me] = choice[...]
    loads[2].start()
    loads[3].start()

    def spread(phase, c, kind):
        source, peer = ((me, sib), (me, cnt), (cnt, sib))[kind]
        return pltpu.make_async_remote_copy(
            src_ref=tokens.at[source, c], dst_ref=tokens.at[source, c],
            send_sem=gather_s.at[phase, kind, c], recv_sem=gather_r.at[phase, kind, c],
            device_id={"expert": peer},
        )

    def normed(values, gain):
        mean_sq = jnp.mean(values * values, axis=-1, keepdims=True)
        return (values * lax.rsqrt(mean_sq + EPSILON) * gain[...]).astype(BF16)

    def pass_on(phase):
        for c in range(CHUNKS):
            spread(phase, c, 1).wait_recv()
            spread(phase, c, 2).start()

    def sent(phase):
        for c in range(CHUNKS):
            for kind in range(3):
                spread(phase, c, kind).wait_send()

    for c in range(CHUNKS):
        hops[c].wait_recv()
        tokens[me, c] = normed(incoming[c].astype(F32), gain_a)
        spread(0, c, 0).start()
        spread(0, c, 1).start()
    pass_on(0)
    for kind in (0, 2):
        for c in range(CHUNKS):
            spread(0, c, kind).wait_recv()
    loads[0].wait()
    n = tokens.shape[0]
    seq = n * block

    @pl.loop(0, qkv.shape[0])
    def _(tile):
        cols = pl.ds(pl.multiple_of(lax.rem(tile, 2) * 256, 256), 256)
        qkv[tile] = jnp.dot(
            tokens[...].reshape(seq, width), vw_in[tile // 2, :, cols],
            preferred_element_type=F32,
        ).astype(BF16)

    span = 256

    @pl.loop(0, heads.shape[1] // HEAD_SIZE)
    def _(head):
        cols = pl.ds(pl.multiple_of(lax.rem(head, 2) * HEAD_SIZE, HEAD_SIZE), HEAD_SIZE)
        place = pl.ds(pl.multiple_of(head * HEAD_SIZE, HEAD_SIZE), HEAD_SIZE)
        for first in range(0, seq, span):
            upto = first + span
            query = qkv[head // 2, first:upto, cols]
            key = qkv[2 + head // 2, :upto, cols]
            value = qkv[4 + head // 2, :upto, cols]
            scores = lax.dot_general(
                query, key, (((1,), (1,)), ((), ())), preferred_element_type=F32
            ) * HEAD_SIZE ** (-0.5)
            row_ids = first + lax.broadcasted_iota(jnp.int32, scores.shape, 0)
            col_ids = lax.broadcasted_iota(jnp.int32, scores.shape, 1)
            scores = jnp.where(col_ids <= row_ids, scores, -jnp.inf)
            powers = jnp.exp(scores - jnp.max(scores, axis=-1, keepdims=True))
            shares = (powers / jnp.sum(powers, axis=-1, keepdims=True)).astype(BF16)
            heads[first:upto, place] = jnp.dot(
                shares, value, preferred_element_type=F32
            ).astype(BF16)

    sent(0)
    loads[1].wait()
    wide = 512

    def reduce_blocks(phase, term, box, buffers):
        to_sib, to_cnt, to_sib_own = buffers
        box_dia, box_sib, box_cnt = box
        moves = []

        def move(kind, c, source, target, peer):
            copy = pltpu.make_async_remote_copy(
                src_ref=source, dst_ref=target, send_sem=sum_s.at[phase, kind, c],
                recv_sem=sum_r.at[phase, kind, c], device_id={"expert": peer},
            )
            copy.start()
            moves.append(copy)
            return copy

        def fill(target, number):
            @pl.loop(0, width // wide)
            def _(j):
                cols = pl.ds(pl.multiple_of(j * wide, wide), wide)
                target[:, :, cols] = term(number, cols).astype(BF16).reshape(CHUNKS, rows, wide)

        fill(to_sib, dia)
        first = move(0, 0, to_sib, box_dia, sib)
        fill(to_cnt, cnt)
        first.wait_recv()
        across = []
        for c in range(CHUNKS):
            to_cnt[c] = (to_cnt[c].astype(F32) + box_dia[c].astype(F32)).astype(BF16)
            across.append(move(1, c, to_cnt.at[c], box_cnt.at[c], cnt))
        fill(to_sib_own, sib)
        beside = move(2, 0, to_sib_own, box_sib, sib)
        return moves, across, beside

    def out_term(number, cols):
        mine = heads[pl.ds(pl.multiple_of(number * block, block), block), :]
        return jnp.dot(mine, vw_out[:, cols], preferred_element_type=F32)

    moves, across, beside = reduce_blocks(
        0, out_term, (stage.at[0], from_sib.at[0], from_cnt.at[0]),
        (packed.at[0], packed.at[1], packed.at[2]),
    )

    @pl.loop(0, width // wide)
    def _(j):
        cols = pl.ds(pl.multiple_of(j * wide, wide), wide)
        own = out_term(me, cols).astype(BF16).astype(F32)
        updated[:, :, cols] = incoming[:, :, cols].astype(F32) + own.reshape(CHUNKS, rows, wide)

    beside.wait_recv()
    for c in range(CHUNKS):
        across[c].wait_recv()
        total = updated[c] + (from_sib[0, c].astype(F32) + from_cnt[0, c].astype(F32))
        updated[c] = total
        tokens[me, c] = normed(total, gain_e)
        spread(1, c, 0).start()
        spread(1, c, 1).start()
    for copy in moves:
        copy.wait_send()
    for copy in shared:
        copy.wait()
    for hop in hops:
        hop.wait_send()

    def dispatch(b):
        names = choices[b]
        own = tokens[b].reshape(block, width)
        gates = jax.nn.sigmoid(
            lax.dot_general(
                columns[...], own, (((1,), (1,)), ((), ())), preferred_element_type=F32
            )
        )
        ids = me * exp_local + lax.broadcasted_iota(jnp.int32, (exp_local, block), 0)
        hit = jnp.zeros((exp_local, block), F32)
        for k in range(names.shape[0]):
            hit = hit + jnp.where(names[k : k + 1, :] == ids, 1.0, 0.0)
        earlier = jnp.where(
            lax.broadcasted_iota(jnp.int32, (block, block), 0)
            < lax.broadcasted_iota(jnp.int32, (block, block), 1), 1.0, 0.0,
        ).astype(BF16)
        place = jnp.dot(hit.astype(BF16), earlier, preferred_element_type=F32)
        place = jnp.where(hit > 0.5, place, -1.0)
        slot = lax.broadcasted_iota(jnp.int32, (exp_local, SLOT, block), 1).astype(F32)
        match = place[:, None, :] == slot
        chosen = jnp.where(match, 1.0, 0.0).reshape(exp_local * SLOT, block).astype(BF16)
        scale = jnp.where(match, gates[:, None, :], 0.0).reshape(exp_local * SLOT, block)
        coarse = scale.astype(BF16)
        weight[b, 0] = coarse
        weight[b, 1] = (scale - coarse.astype(F32)).astype(BF16)

        @pl.loop(0, width // wide)
        def _(j):
            cols = pl.ds(pl.multiple_of(j * wide, wide), wide)
            picked = jnp.dot(
                chosen, tokens[b, :, :, cols].reshape(block, wide), preferred_element_type=F32
            )
            packed[:, b, :, cols] = picked.astype(BF16).reshape(exp_local, SLOT, wide)

    dispatch(me)
    pass_on(1)
    for c in range(CHUNKS):
        spread(1, c, 0).wait_recv()
    dispatch(sib)
    dispatch(cnt)
    for c in range(CHUNKS):
        spread(1, c, 2).wait_recv()
    dispatch(dia)
    loads[2].wait()
    loads[3].wait()

    @pl.loop(0, exp_local)
    def _(e):
        arrived = packed[e].reshape(n * SLOT, width)
        hidden = jnp.maximum(jnp.dot(arrived, ve_in[e], preferred_element_type=F32), 0.0)
        made = jnp.dot(hidden.astype(BF16), ve_out[e], preferred_element_type=F32)
        packed[e] = made.astype(BF16).reshape(n, SLOT, width)

    sent(1)

    def expert_term(number, cols):
        made = packed[:, number, :, cols].reshape(exp_local * SLOT, wide)
        contract = (((0,), (0,)), ((), ()))
        return lax.dot_general(
            weight[number, 0], made, contract, preferred_element_type=F32
        ) + lax.dot_general(weight[number, 1], made, contract, preferred_element_type=F32)

    moves, across, beside = reduce_blocks(
        1, expert_term, (stage.at[1], from_sib.at[1], from_cnt.at[1]),
        (stage.at[0], from_cnt.at[0], from_sib.at[0]),
    )

    @pl.loop(0, width // wide)
    def _(j):
        cols = pl.ds(pl.multiple_of(j * wide, wide), wide)
        updated[:, :, cols] += expert_term(me, cols).reshape(CHUNKS, rows, wide)

    beside.wait_recv()
    for c in range(CHUNKS):
        across[c].wait_recv()
        total = updated[c] + (from_sib[1, c].astype(F32) + from_cnt[1, c].astype(F32))
        out[c] = jnp.where(active[c] > 0, total, incoming[c].astype(F32)).astype(BF16)
    for copy in moves:
        copy.wait_send()


def local_fused(
    carried, halting, section_lap, routing, attention_gain, attention_in, attention_out,
    expert_gain, router, expert_in, expert_out,
):
    tok_dev, width = carried.shape[1:]
    rows = tok_dev // CHUNKS
    n = lax.axis_size("expert")
    exp_local, _, hid = expert_in.shape[1:]
    active = halting[0] >= section_lap[0]
    choice = jnp.where(active[None, :], routing[0].T, -1)
    columns = lax.dynamic_slice_in_dim(
        router[0].T, lax.axis_index("expert") * exp_local, exp_local, 0
    )
    weights_in = jnp.transpose(attention_in[0], (1, 0, 2))
    cols = weights_in.shape[2]
    seq = n * tok_dev
    vmem, far = pl.BlockSpec(memory_space=pltpu.VMEM), pl.BlockSpec(memory_space=pl.ANY)
    tile = (CHUNKS, rows, width)
    dma = pltpu.SemaphoreType.DMA
    result = pl.pallas_call(
        tick_kernel,
        out_shape=jax.ShapeDtypeStruct(tile, BF16),
        in_specs=[far] + [vmem] * 5 + [far] * 4,
        out_specs=vmem,
        scratch_shapes=[
            pltpu.VMEM(weights_in.shape, BF16),
            pltpu.VMEM((cols, width), BF16),
            pltpu.VMEM((exp_local, width, hid), BF16),
            pltpu.VMEM((exp_local, hid, width), BF16),
            pltpu.VMEM((exp_local, n, SLOT, width), BF16),
            pltpu.VMEM(tile, BF16),
            pltpu.VMEM((n,) + tile, BF16),
            pltpu.VMEM(tile, F32),
            pltpu.VMEM((3 * cols // 256, seq, 256), BF16),
            pltpu.VMEM((seq, cols), BF16),
            pltpu.VMEM((2,) + tile, BF16),
            pltpu.VMEM((2,) + tile, BF16),
            pltpu.VMEM((2,) + tile, BF16),
            pltpu.VMEM((n, 2, exp_local * SLOT, tok_dev), BF16),
            pltpu.VMEM((n,) + choice.shape, jnp.int32),
            dma((4,)), dma((CHUNKS,)), dma((CHUNKS,)),
            dma((2, 3, CHUNKS)), dma((2, 3, CHUNKS)),
            dma((2, 3, CHUNKS)), dma((2, 3, CHUNKS)),
            dma((3,)), dma((3,)),
        ],
        compiler_params=pltpu.CompilerParams(
            collective_id=0, has_side_effects=True, vmem_limit_bytes=62 * 1024 * 1024
        ),
        cost_estimate=pl.CostEstimate(
            flops=10 * 10**9, bytes_accessed=45 * 10**6, transcendentals=10**6
        ),
    )(
        carried[0].reshape(tile),
        choice,
        active.astype(jnp.int32).reshape(CHUNKS, rows, 1),
        attention_gain,
        expert_gain,
        columns,
        weights_in,
        attention_out[0],
        expert_in[0],
        expert_out[0],
    )
    return result.reshape(1, tok_dev, width)


def solution(mesh):
    in_specs = (
        P("section", "expert", None),
        P("section", "expert"),
        P("section"),
        P("section", "expert", None),
        P("section", None),
        P("section", None, None, "expert"),
        P("section", "expert", None),
        P("section", None),
        P("section", None, None),
        P("section", "expert", None, None),
        P("section", "expert", None, None),
    )
    out_specs = P("section", "expert", None)
    fused = mesh.shape["expert"] == 4 and mesh.shape["section"] > 2
    local = local_fused if fused else local_general
    return jax.shard_map(local, mesh=mesh, in_specs=in_specs, out_specs=out_specs, check_vma=False)
```

```python
import jax
import jax.numpy as jnp
from jax import lax
from jax.experimental import pallas as pl
from jax.experimental.pallas import tpu as pltpu
from jax.sharding import PartitionSpec as P

HEAD_SIZE = 128
CAP = 24


EPSILON = 1e-06


def passed_along(block, axis, distance):
    devices = range(lax.axis_size(axis))
    route = [((i - distance) % len(devices), i) for i in devices]
    return lax.ppermute(block, axis, route)


def rms_scale(inputs, gain_row):
    mean_sq = jnp.mean(inputs * inputs, axis=-1, keepdims=True)
    return inputs * lax.rsqrt(mean_sq + EPSILON) * gain_row


def local_general(
    carried,
    halting,
    section_lap,
    routing,
    attention_gain,
    attention_in,
    attention_out,
    expert_gain,
    router,
    expert_in,
    expert_out,
):
    incoming = passed_along(carried, "section", 1)[0]
    tok_dev = incoming.shape[0]
    model_width = incoming.shape[1]
    groups = lax.axis_size("expert")
    residual = incoming.astype(jnp.float32)
    normed = rms_scale(residual, attention_gain[0]).astype(jnp.bfloat16)
    weights_in = jnp.transpose(attention_in[0], (1, 0, 2))
    head_cols = weights_in.shape[2]
    heads_here = head_cols // HEAD_SIZE
    gathered = lax.all_gather(normed, "expert", axis=0, tiled=True)
    seq_len = gathered.shape[0]
    queries, keys_all, values_all = (
        jnp.dot(gathered, weights_in[part], preferred_element_type=jnp.float32)
        .astype(jnp.bfloat16)
        .reshape(seq_len, heads_here, HEAD_SIZE)
        for part in range(3)
    )
    row_block = min(512, seq_len)

    def attend_block(block_index):
        first_row = block_index * row_block
        query_rows = lax.dynamic_slice_in_dim(queries, first_row, row_block, 0)
        scores = jnp.einsum(
            "qhc,khc->hqk", query_rows, keys_all, preferred_element_type=jnp.float32
        ) * HEAD_SIZE ** (-0.5)
        row_ids = first_row + lax.broadcasted_iota(jnp.int32, (1, row_block, seq_len), 1)
        col_ids = lax.broadcasted_iota(jnp.int32, (1, row_block, seq_len), 2)
        scores = jnp.where(col_ids <= row_ids, scores, -jnp.inf)
        row_max = jnp.max(scores, axis=-1, keepdims=True)
        weights = jnp.exp(scores - row_max)
        weights = (weights / jnp.sum(weights, axis=-1, keepdims=True)).astype(jnp.bfloat16)
        return jnp.einsum(
            "hqk,khc->qhc", weights, values_all, preferred_element_type=jnp.float32
        ).astype(jnp.bfloat16)

    attended = lax.map(attend_block, jnp.arange(seq_len // row_block, dtype=jnp.int32)).reshape(
        seq_len, head_cols
    )
    out_rows = attention_out[0]
    attention_sum = lax.psum_scatter(
        jnp.dot(attended, out_rows, preferred_element_type=jnp.float32).astype(jnp.bfloat16),
        "expert",
        scatter_dimension=0,
        tiled=True,
    ).astype(jnp.float32)
    updated = residual + attention_sum
    expert_input = rms_scale(updated, expert_gain[0]).astype(jnp.bfloat16)
    active = halting[0] >= section_lap[0]
    experts_total = router.shape[2]
    exp_local = expert_in.shape[1]
    routes = jnp.where(active[:, None], routing[0], experts_total).T
    routes_all = lax.all_gather(routes, "expert", axis=0)
    expert_ids = lax.axis_index("expert") * exp_local + jnp.arange(exp_local, dtype=jnp.int32)
    chosen = jnp.any(routes_all[:, :, None, :] == expert_ids[None, None, :, None], axis=1)
    earlier = jnp.triu(jnp.ones((tok_dev, tok_dev), jnp.bfloat16), 1)
    place = jnp.einsum(
        "bet,tu->beu", chosen.astype(jnp.bfloat16), earlier, preferred_element_type=jnp.float32
    ).astype(jnp.int32)
    slots = jnp.where(chosen, place, CAP)[:, :, None, :] == jnp.arange(CAP)[:, None]
    tokens = lax.all_gather(expert_input, "expert", axis=0)
    columns = lax.dynamic_slice_in_dim(router[0].T, expert_ids[0], exp_local, 0)
    gates = jax.nn.sigmoid(
        jnp.einsum("ed,btd->bet", columns, tokens, preferred_element_type=jnp.float32)
    )
    packed = jnp.einsum(
        "bect,btd->ebcd", slots.astype(jnp.bfloat16), tokens, preferred_element_type=jnp.bfloat16
    ).reshape(exp_local, groups * CAP, model_width)
    hidden = jax.nn.relu(
        jnp.einsum("ecd,edh->ech", packed, expert_in[0], preferred_element_type=jnp.float32)
    ).astype(jnp.bfloat16)
    produced = jnp.einsum(
        "ech,ehd->ecd", hidden, expert_out[0], preferred_element_type=jnp.float32
    ).astype(jnp.bfloat16)
    produced = produced.reshape(exp_local, groups, CAP, model_width)
    weight = jnp.where(slots, gates[:, :, None, :], 0.0)
    coarse = lax.reduce_precision(weight, 8, 7)
    fine = (weight - coarse).astype(jnp.bfloat16)
    partial = sum(
        jnp.einsum("bect,ebcd->btd", part, produced, preferred_element_type=jnp.float32)
        for part in (coarse.astype(jnp.bfloat16), fine)
    )
    expert_sum = lax.psum_scatter(
        partial.astype(jnp.bfloat16).reshape(-1, model_width),
        "expert",
        scatter_dimension=0,
        tiled=True,
    ).astype(jnp.float32)
    stepped = jnp.where(active[:, None], updated + expert_sum, residual).astype(jnp.bfloat16)
    return stepped[None]


CHUNKS = 4
SLOT = 32
F32 = jnp.float32
BF16 = jnp.bfloat16


def tick_kernel(
    carried, routes, halts, lap, active, gain_a, gain_e, router_rows, w_in, w_out, e_in, e_out, out,
    vw_in, vw_out, ve_in, ve_out, packed, incoming, tokens, updated, qkv, heads,
    stage, from_sib, from_cnt, weight, choices,
    load_sem, hop_s, hop_r, gather_s, gather_r, sum_s, sum_r, choice_s, choice_r,
):
    me = lax.axis_index("expert")
    section, sections = lax.axis_index("section"), lax.axis_size("section")
    sib = me + 1 - 2 * lax.rem(me, 2)
    cnt = me + 2 - 4 * (me // 2)
    dia = sib + 2 - 4 * (sib // 2)
    after, ahead = lax.rem(section + 1, sections), lax.rem(section + sections - 1, sections)
    exp_local, width = e_in.shape[0], e_in.shape[1]
    rows = tokens.shape[2]
    block = CHUNKS * rows

    loads = [
        pltpu.make_async_copy(w_in, vw_in, load_sem.at[0]),
        pltpu.make_async_copy(w_out, vw_out, load_sem.at[1]),
        pltpu.make_async_copy(e_in, ve_in, load_sem.at[2]),
        pltpu.make_async_copy(e_out, ve_out, load_sem.at[3]),
    ]
    loads[0].start()
    loads[1].start()

    barrier = pltpu.get_barrier_semaphore()
    for peer in (sib, cnt, dia):
        pl.semaphore_signal(barrier, inc=1, device_id={"expert": peer})
    for peer in (after, ahead):
        pl.semaphore_signal(barrier, inc=1, device_id={"section": peer})
    pl.semaphore_wait(barrier, 5)

    hops = [
        pltpu.make_async_remote_copy(
            src_ref=carried.at[c], dst_ref=incoming.at[c], send_sem=hop_s.at[c],
            recv_sem=hop_r.at[c], device_id={"section": after},
        )
        for c in range(CHUNKS)
    ]
    for hop in hops:
        hop.start()
    choices[me] = jnp.where(halts[...] >= lap[...], routes[...], -1)
    shared = []
    for i, peer in enumerate((sib, cnt, dia)):
        shared.append(
            pltpu.make_async_remote_copy(
                src_ref=choices.at[me], dst_ref=choices.at[me], send_sem=choice_s.at[i],
                recv_sem=choice_r.at[i], device_id={"expert": peer},
            )
        )
        shared[-1].start()
    loads[2].start()
    loads[3].start()

    def spread(phase, c, kind):
        source, peer = ((me, sib), (me, cnt), (cnt, sib))[kind]
        return pltpu.make_async_remote_copy(
            src_ref=tokens.at[source, c], dst_ref=tokens.at[source, c],
            send_sem=gather_s.at[phase, kind, c], recv_sem=gather_r.at[phase, kind, c],
            device_id={"expert": peer},
        )

    def normed(values, gain):
        mean_sq = jnp.mean(values * values, axis=-1, keepdims=True)
        return (values * lax.rsqrt(mean_sq + EPSILON) * gain[...]).astype(BF16)

    def pass_on(phase):
        for c in range(CHUNKS):
            spread(phase, c, 1).wait_recv()
            spread(phase, c, 2).start()

    def sent(phase):
        for c in range(CHUNKS):
            for kind in range(3):
                spread(phase, c, kind).wait_send()

    for c in range(CHUNKS):
        hops[c].wait_recv()
        tokens[me, c] = normed(incoming[c].astype(F32), gain_a)
        spread(0, c, 0).start()
        spread(0, c, 1).start()
    pass_on(0)
    for kind in (0, 2):
        for c in range(CHUNKS):
            spread(0, c, kind).wait_recv()
    loads[0].wait()
    n = tokens.shape[0]
    seq = n * block

    @pl.loop(0, qkv.shape[0])
    def _(tile):
        cols = pl.ds(pl.multiple_of(lax.rem(tile, 2) * 256, 256), 256)
        qkv[tile] = jnp.dot(
            tokens[...].reshape(seq, width), vw_in[tile // 2, :, cols],
            preferred_element_type=F32,
        ).astype(BF16)

    span = 256

    @pl.loop(0, heads.shape[1] // HEAD_SIZE, unroll=2)
    def _(head):
        cols = pl.ds(pl.multiple_of(lax.rem(head, 2) * HEAD_SIZE, HEAD_SIZE), HEAD_SIZE)
        place = pl.ds(pl.multiple_of(head * HEAD_SIZE, HEAD_SIZE), HEAD_SIZE)
        for first in range(0, seq, span):
            upto = first + span
            query = qkv[head // 2, first:upto, cols]
            key = qkv[2 + head // 2, :upto, cols]
            value = qkv[4 + head // 2, :upto, cols]
            scores = lax.dot_general(
                query, key, (((1,), (1,)), ((), ())), preferred_element_type=F32
            ) * HEAD_SIZE ** (-0.5)
            row_ids = first + lax.broadcasted_iota(jnp.int32, scores.shape, 0)
            col_ids = lax.broadcasted_iota(jnp.int32, scores.shape, 1)
            scores = jnp.where(col_ids <= row_ids, scores, -jnp.inf)
            powers = jnp.exp(scores - jnp.max(scores, axis=-1, keepdims=True))
            shares = (powers * (1.0 / jnp.sum(powers, axis=-1, keepdims=True))).astype(BF16)
            heads[first:upto, place] = jnp.dot(
                shares, value, preferred_element_type=F32
            ).astype(BF16)

    sent(0)
    loads[1].wait()
    wide = 512

    def reduce_blocks(phase, term, box, buffers):
        to_sib, to_cnt, to_sib_own = buffers
        box_dia, box_sib, box_cnt = box
        moves = []

        def move(kind, c, source, target, peer):
            copy = pltpu.make_async_remote_copy(
                src_ref=source, dst_ref=target, send_sem=sum_s.at[phase, kind, c],
                recv_sem=sum_r.at[phase, kind, c], device_id={"expert": peer},
            )
            copy.start()
            moves.append(copy)
            return copy

        def fill(target, number):
            @pl.loop(0, width // wide)
            def _(j):
                cols = pl.ds(pl.multiple_of(j * wide, wide), wide)
                target[:, :, cols] = term(number, cols).astype(BF16).reshape(CHUNKS, rows, wide)

        fill(to_sib, dia)
        first = move(0, 0, to_sib, box_dia, sib)
        fill(to_cnt, cnt)
        first.wait_recv()
        across = []
        for c in range(CHUNKS):
            to_cnt[c] = (to_cnt[c].astype(F32) + box_dia[c].astype(F32)).astype(BF16)
            across.append(move(1, c, to_cnt.at[c], box_cnt.at[c], cnt))
        fill(to_sib_own, sib)
        beside = move(2, 0, to_sib_own, box_sib, sib)
        return moves, across, beside

    def out_term(number, cols):
        mine = heads[pl.ds(pl.multiple_of(number * block, block), block), :]
        return jnp.dot(mine, vw_out[:, cols], preferred_element_type=F32)

    moves, across, beside = reduce_blocks(
        0, out_term, (stage.at[0], from_sib.at[0], from_cnt.at[0]),
        (packed.at[0], packed.at[1], packed.at[2]),
    )

    @pl.loop(0, width // wide)
    def _(j):
        cols = pl.ds(pl.multiple_of(j * wide, wide), wide)
        own = out_term(me, cols).astype(BF16).astype(F32)
        updated[:, :, cols] = incoming[:, :, cols].astype(F32) + own.reshape(CHUNKS, rows, wide)

    beside.wait_recv()
    for c in range(CHUNKS):
        across[c].wait_recv()
        total = updated[c] + (from_sib[0, c].astype(F32) + from_cnt[0, c].astype(F32))
        updated[c] = total
        tokens[me, c] = normed(total, gain_e)
        spread(1, c, 0).start()
        spread(1, c, 1).start()
    for copy in moves:
        copy.wait_send()
    for copy in shared:
        copy.wait()
    for hop in hops:
        hop.wait_send()

    columns = router_rows[pl.ds(pl.multiple_of(me * exp_local, exp_local), exp_local), :]

    def dispatch(b):
        names = choices[b]
        own = tokens[b].reshape(block, width)
        gates = jax.nn.sigmoid(
            lax.dot_general(
                columns, own, (((1,), (1,)), ((), ())), preferred_element_type=F32
            )
        )
        ids = me * exp_local + lax.broadcasted_iota(jnp.int32, (exp_local, block), 0)
        hit = jnp.zeros((exp_local, block), F32)
        for k in range(names.shape[0]):
            hit = hit + jnp.where(names[k : k + 1, :] == ids, 1.0, 0.0)
        earlier = jnp.where(
            lax.broadcasted_iota(jnp.int32, (block, block), 0)
            < lax.broadcasted_iota(jnp.int32, (block, block), 1), 1.0, 0.0,
        ).astype(BF16)
        place = jnp.dot(hit.astype(BF16), earlier, preferred_element_type=F32)
        place = jnp.where(hit > 0.5, place, -1.0)
        slot = lax.broadcasted_iota(jnp.int32, (exp_local, SLOT, block), 1).astype(F32)
        match = place[:, None, :] == slot
        chosen = jnp.where(match, 1.0, 0.0).reshape(exp_local * SLOT, block).astype(BF16)
        scale = jnp.where(match, gates[:, None, :], 0.0).reshape(exp_local * SLOT, block).T
        coarse = scale.astype(BF16)
        weight[b, :block] = coarse
        weight[b, block:] = (scale - coarse.astype(F32)).astype(BF16)

        @pl.loop(0, width // wide)
        def _(j):
            cols = pl.ds(pl.multiple_of(j * wide, wide), wide)
            picked = jnp.dot(
                chosen, tokens[b, :, :, cols].reshape(block, wide), preferred_element_type=F32
            )
            packed[:, b, :, cols] = picked.astype(BF16).reshape(exp_local, SLOT, wide)

    dispatch(me)
    pass_on(1)
    for c in range(CHUNKS):
        spread(1, c, 0).wait_recv()
    dispatch(sib)
    dispatch(cnt)
    for c in range(CHUNKS):
        spread(1, c, 2).wait_recv()
    dispatch(dia)
    loads[2].wait()
    loads[3].wait()

    @pl.loop(0, exp_local, unroll=2)
    def _(e):
        arrived = packed[e].reshape(n * SLOT, width)
        hidden = jnp.maximum(jnp.dot(arrived, ve_in[e], preferred_element_type=F32), 0.0)
        made = jnp.dot(hidden.astype(BF16), ve_out[e], preferred_element_type=F32)
        packed[e] = made.astype(BF16).reshape(n, SLOT, width)

    sent(1)

    def expert_term(number, cols):
        made = packed[:, number, :, cols].reshape(exp_local * SLOT, wide)
        both = jnp.dot(weight[number], made, preferred_element_type=F32)
        return both[:block] + both[block:]

    moves, across, beside = reduce_blocks(
        1, expert_term, (stage.at[1], from_sib.at[1], from_cnt.at[1]),
        (stage.at[0], from_cnt.at[0], from_sib.at[0]),
    )

    @pl.loop(0, width // wide)
    def _(j):
        cols = pl.ds(pl.multiple_of(j * wide, wide), wide)
        updated[:, :, cols] += expert_term(me, cols).reshape(CHUNKS, rows, wide)

    beside.wait_recv()
    for c in range(CHUNKS):
        across[c].wait_recv()
        total = updated[c] + (from_sib[1, c].astype(F32) + from_cnt[1, c].astype(F32))
        out[c] = jnp.where(active[c] > 0, total, incoming[c].astype(F32)).astype(BF16)
    for copy in moves:
        copy.wait_send()


def local_fused(
    carried, halting, section_lap, routing, attention_gain, attention_in, attention_out,
    expert_gain, router, expert_in, expert_out,
):
    tok_dev, width = carried.shape[1:]
    rows = tok_dev // CHUNKS
    n = lax.axis_size("expert")
    exp_local, _, hid = expert_in.shape[1:]
    active = halting[0] >= section_lap[0]
    weights_in = jnp.transpose(attention_in[0], (1, 0, 2))
    cols = weights_in.shape[2]
    seq = n * tok_dev
    vmem, far = pl.BlockSpec(memory_space=pltpu.VMEM), pl.BlockSpec(memory_space=pl.ANY)
    tile = (CHUNKS, rows, width)
    dma = pltpu.SemaphoreType.DMA
    result = pl.pallas_call(
        tick_kernel,
        out_shape=jax.ShapeDtypeStruct(tile, BF16),
        in_specs=[far] + [vmem] * 7 + [far] * 4,
        out_specs=vmem,
        scratch_shapes=[
            pltpu.VMEM(weights_in.shape, BF16),
            pltpu.VMEM((cols, width), BF16),
            pltpu.VMEM((exp_local, width, hid), BF16),
            pltpu.VMEM((exp_local, hid, width), BF16),
            pltpu.VMEM((exp_local, n, SLOT, width), BF16),
            pltpu.VMEM(tile, BF16),
            pltpu.VMEM((n,) + tile, BF16),
            pltpu.VMEM(tile, F32),
            pltpu.VMEM((3 * cols // 256, seq, 256), BF16),
            pltpu.VMEM((seq, cols), BF16),
            pltpu.VMEM((2,) + tile, BF16),
            pltpu.VMEM((2,) + tile, BF16),
            pltpu.VMEM((2,) + tile, BF16),
            pltpu.VMEM((n, 2 * tok_dev, exp_local * SLOT), BF16),
            pltpu.VMEM((n, routing.shape[2], tok_dev), jnp.int32),
            dma((4,)), dma((CHUNKS,)), dma((CHUNKS,)),
            dma((2, 3, CHUNKS)), dma((2, 3, CHUNKS)),
            dma((2, 3, CHUNKS)), dma((2, 3, CHUNKS)),
            dma((3,)), dma((3,)),
        ],
        compiler_params=pltpu.CompilerParams(
            collective_id=0, has_side_effects=True, vmem_limit_bytes=62 * 1024 * 1024
        ),
        cost_estimate=pl.CostEstimate(
            flops=10 * 10**9, bytes_accessed=45 * 10**6, transcendentals=10**6
        ),
    )(
        carried[0].reshape(tile),
        routing[0].T,
        halting,
        section_lap.reshape(1, 1),
        active.astype(jnp.int32).reshape(CHUNKS, rows, 1),
        attention_gain,
        expert_gain,
        router[0].T,
        weights_in,
        attention_out[0],
        expert_in[0],
        expert_out[0],
    )
    return result.reshape(1, tok_dev, width)


def solution(mesh):
    in_specs = (
        P("section", "expert", None),
        P("section", "expert"),
        P("section"),
        P("section", "expert", None),
        P("section", None),
        P("section", None, None, "expert"),
        P("section", "expert", None),
        P("section", None),
        P("section", None, None),
        P("section", "expert", None, None),
        P("section", "expert", None, None),
    )
    out_specs = P("section", "expert", None)
    fused = mesh.shape["expert"] == 4 and mesh.shape["section"] > 2
    local = local_fused if fused else local_general
    return jax.shard_map(local, mesh=mesh, in_specs=in_specs, out_specs=out_specs, check_vma=False)
```
